128 devices in a mesh: node: 16 (over x, z), local: 8 (over y, core).
Axes of the slice: x: 4, y: 4, z: 4, core: 2. Of those that a mesh axis runs over, the one named last changes fastest.
Arguments:
- tokens: bfloat16 [16384, 2880], P(('node', 'local')), may hold values from -6 to 6
- out_grad: bfloat16 [16384, 2880], P(('node', 'local')), may hold values from -2.390625 to 2.390625
- routes: int32 [16384, 4], P(('node', 'local')), may hold values from 0 to 127, all different within a row; in each aligned block of 128 rows (0 to 127, 128 to 255, ...) at most 5 rows name the same one
- gates: float32 [16384, 4], P(('node', 'local')), may hold values from 0.1 to 1
- w_gate: bfloat16 [128, 2880, 1440], P(('node', 'local')), may hold values from -0.109375 to 0.109375
- w_up: bfloat16 [128, 2880, 1440], P(('node', 'local')), may hold values from -0.109375 to 0.109375
- w_down: bfloat16 [128, 1440, 2880], P(('node', 'local')), may hold values from -0.15625 to 0.15625
Outputs:
- input_grad: bfloat16 [16384, 2880], P(('node', 'local'))
- gate_grad: float32 [16384, 4], P(('node', 'local'))
The draws below stay inside these ranges and needn't reach their ends.
Inputs may be any that keep to these rules, and one draw needn't show every extreme that they name: Each token names 4 different experts. Among the 128 tokens of one device (aligned blocks of rows), no expert is named by more than 5 routes, and in some such block some expert is named by exactly 5.
All inputs are finite; a program needn't handle non-finite values.
Results may differ from the reference program's by a relative error of at most 0.005.
Values may be sent and summed in bfloat16 or wider, within the bound.
No kernel may reach another device: no remote copies, remote signals or barrier semaphores. Data moves between devices by JAX's collectives and lax.ppermute only.
A program may use at most 128 MiB of HBM per device.

```python
import math
import jax
import jax.numpy as jnp
import numpy as np
from jax import lax

D = 2880
TOPK = 4
FF = 1440
TOK_DEV = 128
EXPERTS = 128
SLOTS = 5
TOKENS = 16384
N_NODE = 16
N_LOCAL = 8


def shard_levels(stream_key, dims, cuts, least, top_value):
    loudness = 1.0
    for position, shards_of in cuts:
        draws = jax.random.uniform(jax.random.fold_in(jax.random.fold_in(stream_key, 6), position), (shards_of,), jnp.float32, least / len(cuts), top_value / len(cuts))
        loudness = loudness * jnp.repeat(jnp.exp(draws), dims[position] // shards_of).reshape((-1,) + (1,) * (len(dims) - 1 - position))
    return loudness


def deal_out(rng, own, number, rows, number_of, top, reach, lean):
    sequence = jax.random.permutation(rng, number_of)
    heavy_load, usual = shares(number_of, rows * top, reach, lean, True), shares(number_of, rows * top, reach, lean, False)
    places = jnp.arange(number_of)

    def named(tallies, offset_by):
        used = int((tallies > 0).sum())
        fixed = max(1, used // 4)
        shifted = fixed + (places - fixed + offset_by * (used - fixed)) % max(1, number_of - fixed)
        return jnp.zeros((number_of,), jnp.int32).at[sequence[jnp.where(places < fixed, places, shifted)]].set(jnp.asarray(tallies, jnp.int32))

    tallies = jnp.where(number % 4 == 0, named(heavy_load, number // 4), named(usual, number - number // 4 - 1))
    mixed = jax.random.permutation(jax.random.fold_in(own, 3), number_of)
    giver, taker = mixed[0:number_of // 2 * 2:2], mixed[1:number_of // 2 * 2:2]
    slack = jnp.minimum(tallies[giver] - 1, reach - tallies[taker]) // 2
    slack = jnp.where((giver == sequence[0]) | (taker == sequence[0]) | (tallies[taker] == 0), 0, jnp.maximum(slack, 0))
    shifted = jax.random.randint(jax.random.fold_in(own, 4), (number_of // 2,), 0, 1 << 20) % (slack + 1)
    tallies = tallies.at[giver].add(-shifted).at[taker].add(shifted)
    members = jnp.searchsorted(jnp.cumsum(tallies), jnp.arange(rows * top), side="right").astype(jnp.int32)
    listing = members.reshape(top, rows).T
    listing = listing[jax.random.permutation(jax.random.fold_in(own, 1), rows)]
    offset_by = jax.random.randint(jax.random.fold_in(own, 2), (rows, 1), 0, top)
    return jnp.take_along_axis(listing, (jnp.arange(top)[None, :] + offset_by) % top, axis=1)


def shares(amount, total, most, slope, full):
    weights = [(1 << 20) // math.isqrt(standing ** slope) + 1 for standing in range(1, amount + 1)]
    largest = most if full else min(most, max(-(-total // amount), total * weights[0] // sum(weights)))
    least = 1 if total - largest >= amount - 1 else 0
    counts, rest = [largest] + [least] * (amount - 1), total - largest - least * (amount - 1)
    while rest > 0:
        movable = [i for i in range(1, amount) if counts[i] < largest] or [i for i in range(1, amount) if counts[i] < most]
        pool, left = sum([weights[i] for i in movable]), rest
        for i in movable:
            more = min(most - counts[i], max(1, left * weights[i] // pool), rest)
            counts[i] = counts[i] + more
            rest = rest - more
    return np.array(counts)


def normal_values(rng, extent, spread, most, split=(), kind=jnp.bfloat16):
    factor_of = shard_levels(rng, extent, split, -0.22, 0.18) if split else 1.0
    drawn = jax.random.normal(rng, extent, jnp.float32) * spread * factor_of
    return jnp.minimum(jnp.maximum(drawn, -most), most).astype(kind)


def setup_inputs(seed: int = 0) -> dict:
    arg_keys = jax.random.split(jax.random.key(seed), 8)
    tokens = normal_values(arg_keys[0], (TOKENS, D), 1.0, 6.0, ((0, 128),))
    out_grad = normal_values(arg_keys[1], (TOKENS, D), 0.4, 2.390625, ((0, 128),))
    routes_keys = jax.random.split(jax.random.fold_in(arg_keys[2], 1), TOKENS // TOK_DEV)
    routes_turns = jax.random.permutation(jax.random.fold_in(arg_keys[2], 3), TOKENS // TOK_DEV)
    routes = jax.vmap(lambda own, number: deal_out(jax.random.fold_in(arg_keys[2], 2), own, number, TOK_DEV, EXPERTS, TOPK, SLOTS, 2))(routes_keys, routes_turns).reshape((TOKENS, TOPK))
    gates = jnp.clip(jnp.exp(math.log(1.0) - 2.3025851 * jax.random.uniform(arg_keys[3], (TOKENS, TOPK), jnp.float32) ** shard_levels(arg_keys[3], (TOKENS, TOPK), ((0, 128),), -0.2, 0.2)), 0.1, 1.0)
    w_gate = normal_values(arg_keys[4], (EXPERTS, D, FF), D ** -0.5, 0.109375, ((0, 128),))
    w_up = normal_values(arg_keys[5], (EXPERTS, D, FF), D ** -0.5, 0.109375, ((0, 128),))
    w_down = normal_values(arg_keys[6], (EXPERTS, FF, D), FF ** -0.5, 0.15625, ((0, 128),))
    return {"tokens": tokens, "out_grad": out_grad, "routes": routes, "gates": gates, "w_gate": w_gate, "w_up": w_up, "w_down": w_down}


def route_ranks(flat_routes):
    count = flat_routes.shape[0]
    same = flat_routes[:, None] == flat_routes[None, :]
    earlier = jnp.arange(count, dtype=jnp.int32)[:, None] > jnp.arange(count, dtype=jnp.int32)[None, :]
    return jnp.sum((same & earlier).astype(jnp.int32), axis=1).astype(jnp.int32)


def expert_backward(rows_in, grads_in, gate_w, up_w, down_w):
    gate_pre = jnp.dot(rows_in, gate_w, preferred_element_type=jnp.float32)
    up_pre = jnp.dot(rows_in, up_w, preferred_element_type=jnp.float32)
    gate_sig = jax.nn.sigmoid(gate_pre)
    gate_act = gate_pre * gate_sig
    hidden = (gate_act * up_pre).astype(jnp.bfloat16)
    expert_out = jnp.dot(hidden, down_w, preferred_element_type=jnp.float32)
    scores = jnp.sum(grads_in.astype(jnp.float32) * expert_out, axis=1)
    contract = (((1,), (1,)), ((), ()))
    hidden_grad = lax.dot_general(grads_in, down_w, contract, preferred_element_type=jnp.float32)
    up_grad = (hidden_grad * gate_act).astype(jnp.bfloat16)
    pre_grad = (hidden_grad * up_pre * gate_sig * (1.0 + gate_pre * (1.0 - gate_sig))).astype(jnp.bfloat16)
    returned = lax.dot_general(pre_grad, gate_w, contract, preferred_element_type=jnp.float32)
    returned = returned + lax.dot_general(up_grad, up_w, contract, preferred_element_type=jnp.float32)
    return returned, scores


def reference(tokens, out_grad, routes, gates, w_gate, w_up, w_down):
    experts = N_NODE * N_LOCAL
    count = TOK_DEV * TOPK
    width = experts * SLOTS
    blocks = routes.reshape(experts, count).astype(jnp.int32)
    ranks = jax.vmap(route_ranks)(blocks)
    owner = jnp.arange(experts, dtype=jnp.int32)[:, None]
    column = owner * SLOTS + ranks
    route_id = owner * count + jnp.arange(count, dtype=jnp.int32)[None, :]
    table = jnp.full((experts, width), -1, dtype=jnp.int32).at[blocks, column].set(route_id)
    flat_gates = gates.reshape(-1)

    def visit(carry, item):
        input_acc, gate_acc = carry
        route_ids, gate_w, up_w, down_w = item
        valid = route_ids >= 0
        safe_ids = jnp.maximum(route_ids, 0).astype(jnp.int32)
        token_rows = (safe_ids // TOPK).astype(jnp.int32)
        rows_in = jnp.where(valid[:, None], tokens[token_rows], jnp.zeros((), tokens.dtype))
        grads_in = jnp.where(valid[:, None], out_grad[token_rows], jnp.zeros((), out_grad.dtype))
        returned, scores = expert_backward(rows_in, grads_in, gate_w, up_w, down_w)
        weights = jnp.where(valid, flat_gates[safe_ids], jnp.zeros((), flat_gates.dtype))
        input_acc = input_acc.at[token_rows].add(weights[:, None] * returned)
        gate_acc = gate_acc.at[safe_ids].add(jnp.where(valid, scores, jnp.zeros((), scores.dtype)))
        return (input_acc, gate_acc), None

    start = (jnp.zeros((tokens.shape[0], tokens.shape[1]), jnp.float32), jnp.zeros(flat_gates.shape, jnp.float32))
    (input_acc, gate_acc), _ = lax.scan(visit, start, (table, w_gate, w_up, w_down))
    return input_acc.astype(jnp.bfloat16), gate_acc.reshape(gates.shape)
```

```python
import functools

import jax
import jax.numpy as jnp
from jax import lax
from jax.experimental import pallas as pl
from jax.experimental.pallas import tpu as pltpu
from jax.sharding import PartitionSpec as P

LANES = 128
GROUP = 16
SLOTS = 5
BF = jnp.bfloat16
F32 = jnp.float32
NT = (((1,), (1,)), ((), ()))
VMEM_LIMIT = 60 * 1024 * 1024


def round_up(value, step):
    return -(-value // step) * step


def route_maps(routes_t):
    topk, tokens = routes_t.shape
    expert = lax.broadcasted_iota(jnp.int32, (LANES, tokens), 0)
    named = [jnp.where(routes_t[k : k + 1, :] == expert, 1.0, 0.0) for k in range(topk)]
    total = functools.reduce(lambda a, b: a + b, named)
    row = lax.broadcasted_iota(jnp.int32, (tokens, tokens), 0)
    column = lax.broadcasted_iota(jnp.int32, (tokens, tokens), 1)
    earlier = jnp.where(row < column, 1.0, 0.0).astype(BF)
    rank = jnp.dot(total.astype(BF), earlier, preferred_element_type=F32)
    return named, total, rank


def pack_rows(step, load, stage_ref, out_ref, tensors, tiles, pitch):
    base = pl.multiple_of(step * GROUP, GROUP)
    for j in range(tensors):
        for s in range(SLOTS):
            for t in range(tiles):
                value = load(j, pl.ds(s * LANES + base, GROUP), slice(t * LANES, (t + 1) * LANES))
                stage_ref[pl.ds((j * SLOTS + s) * tiles + t, GROUP, stride=pitch), :] = value.astype(F32)
    rows = out_ref.shape[1]
    for a in range(GROUP):
        out_ref[a] = stage_ref[a * pitch : a * pitch + rows, :].astype(BF)


def unpack_rows(step, in_ref, stage_ref, store, tensors, tiles, pitch):
    base = pl.multiple_of(step * GROUP, GROUP)
    rows = in_ref.shape[1]
    for a in range(GROUP):
        stage_ref[a * pitch : a * pitch + rows, :] = in_ref[a].astype(F32)
    for j in range(tensors):
        for s in range(SLOTS):
            for t in range(tiles):
                value = stage_ref[pl.ds((j * SLOTS + s) * tiles + t, GROUP, stride=pitch), :]
                store(j, pl.ds(s * LANES + base, GROUP), slice(t * LANES, (t + 1) * LANES), value.astype(BF))


def dispatch_kernel(tiles, pitch, routes_ref, tok_ref, grad_ref, out_ref, rows_ref, stage_ref):
    step = pl.program_id(0)
    features = tok_ref.shape[0]

    @pl.when(step == 0)
    def _():
        stage_ref[...] = jnp.zeros_like(stage_ref)
        rows_ref[:, :, (tiles - 1) * LANES :] = jnp.zeros((2, SLOTS * LANES, LANES), BF)
        _, total, rank = route_maps(routes_ref[...])
        place = jnp.concatenate(
            [jnp.where(rank == float(s), total, 0.0).astype(BF) for s in range(SLOTS)], axis=0
        )
        for j, ref in enumerate((tok_ref, grad_ref)):
            for lo in range(0, features, 512):
                hi = min(lo + 512, features)
                part = lax.dot_general(place, ref[lo:hi, :], NT, preferred_element_type=F32)
                rows_ref[j, :, lo:hi] = part.astype(BF)

    pack_rows(step, lambda j, r, c: rows_ref[j, r, c], stage_ref, out_ref, 2, tiles, pitch)


def dispatch(routes_t, tok_t, grad_t):
    features, tokens = tok_t.shape
    tiles = -(-features // LANES)
    rows = round_up(2 * SLOTS * tiles, 8)
    pitch = rows + 1
    return pl.pallas_call(
        functools.partial(dispatch_kernel, tiles, pitch),
        grid=(LANES // GROUP,),
        in_specs=[
            pl.BlockSpec(routes_t.shape, lambda i: (0, 0)),
            pl.BlockSpec(tok_t.shape, lambda i: (0, 0)),
            pl.BlockSpec(grad_t.shape, lambda i: (0, 0)),
        ],
        out_specs=pl.BlockSpec((GROUP, rows, LANES), lambda i: (i, 0, 0)),
        out_shape=jax.ShapeDtypeStruct((LANES, rows, LANES), BF),
        scratch_shapes=[
            pltpu.VMEM((2, SLOTS * LANES, tiles * LANES), BF),
            pltpu.VMEM((GROUP * pitch, LANES), F32),
        ],
        compiler_params=pltpu.CompilerParams(vmem_limit_bytes=VMEM_LIMIT),
    )(routes_t, tok_t, grad_t)


def expert_kernel(
    tiles, pitch_in, pitch_out, in_ref, gate_hbm, up_hbm, down_hbm, out_ref,
    rows_ref, back_ref, pre_ref, upg_ref, gate_ref, up_ref, down_ref, stage_ref, stage_out_ref, sems,
):
    step = pl.program_id(0)
    steps = LANES // GROUP
    hidden, features = gate_hbm.shape
    copies = [
        pltpu.make_async_copy(src, dst, sems.at[i])
        for i, (src, dst) in enumerate(((gate_hbm, gate_ref), (up_hbm, up_ref), (down_hbm, down_ref)))
    ]

    @pl.when(step == 0)
    def _():
        for copy in copies:
            copy.start()

    @pl.when(step < steps)
    def _():
        def store(j, r, c, value):
            rows_ref[j, r, c] = value

        unpack_rows(step, in_ref, stage_ref, store, 2, tiles, pitch_in)

    @pl.when(step == steps - 1)
    def _():
        stage_out_ref[...] = jnp.zeros_like(stage_out_ref)
        for copy in copies:
            copy.wait()
        tok = rows_ref.at[0]
        grad = rows_ref.at[1]
        score = jnp.zeros((SLOTS * LANES, 1), F32)
        for lo in range(0, hidden, 512):
            hi = min(lo + 512, hidden)
            x = tok[:, :features]
            gate_pre = lax.dot_general(x, gate_ref[lo:hi, :], NT, preferred_element_type=F32)
            up_pre = lax.dot_general(x, up_ref[lo:hi, :], NT, preferred_element_type=F32)
            hidden_grad = lax.dot_general(
                grad[:, :features], down_ref[lo:hi, :], NT, preferred_element_type=F32
            )
            sig = jax.nn.sigmoid(gate_pre)
            act = gate_pre * sig
            act_up = (act * up_pre).astype(BF).astype(F32)
            score = score + jnp.sum(act_up * hidden_grad, axis=1, keepdims=True)
            upg_ref[:, lo:hi] = (hidden_grad * act).astype(BF)
            pre_ref[:, lo:hi] = (hidden_grad * up_pre * sig * (1.0 + gate_pre * (1.0 - sig))).astype(BF)
        high = score.astype(BF)
        low = (score - high.astype(F32)).astype(BF)
        whole = features // 256

        def columns(lo, width):
            back = jnp.dot(pre_ref[...], gate_ref[:, pl.ds(lo, width)], preferred_element_type=F32)
            return back + jnp.dot(upg_ref[...], up_ref[:, pl.ds(lo, width)], preferred_element_type=F32)

        @pl.loop(0, whole)
        def _(n):
            lo = pl.multiple_of(n * 256, 256)
            back_ref[:, pl.ds(lo, 256)] = columns(lo, 256).astype(BF)

        rest = features - whole * 256
        lane = lax.broadcasted_iota(jnp.int32, (SLOTS * LANES, LANES), 1)
        last = jnp.where(lane == rest, high.astype(F32), jnp.where(lane == rest + 1, low.astype(F32), 0.0))
        back_ref[:, whole * 256 :] = last.astype(BF)
        back_ref[:, whole * 256 : features] = columns(whole * 256, rest).astype(BF)

    @pl.when(step >= steps)
    def _():
        pack_rows(step - steps, lambda j, r, c: back_ref[r, c], stage_out_ref, out_ref, 1, tiles, pitch_out)


def expert(recv, gate_t, up_t, down):
    peers, rows_in, _ = recv.shape
    hidden, features = gate_t.shape
    tiles = -(-features // LANES)
    rows_out = round_up(SLOTS * tiles, 8)
    steps = LANES // GROUP
    pitch_in, pitch_out = rows_in + 1, rows_out + 1
    wide = SLOTS * LANES
    flops = 5 * 2 * wide * hidden * features
    return pl.pallas_call(
        functools.partial(expert_kernel, tiles, pitch_in, pitch_out),
        grid=(2 * steps,),
        in_specs=[
            pl.BlockSpec((GROUP, rows_in, LANES), lambda i: (jnp.minimum(i, steps - 1), 0, 0)),
            pl.BlockSpec(memory_space=pl.ANY),
            pl.BlockSpec(memory_space=pl.ANY),
            pl.BlockSpec(memory_space=pl.ANY),
        ],
        out_specs=pl.BlockSpec((GROUP, rows_out, LANES), lambda i: (jnp.maximum(i - steps, 0), 0, 0)),
        out_shape=jax.ShapeDtypeStruct((peers, rows_out, LANES), BF),
        scratch_shapes=[
            pltpu.VMEM((2, wide, tiles * LANES), BF),
            pltpu.VMEM((wide, tiles * LANES), BF),
            pltpu.VMEM((wide, hidden), BF),
            pltpu.VMEM((wide, hidden), BF),
            pltpu.VMEM((hidden, features), BF),
            pltpu.VMEM((hidden, features), BF),
            pltpu.VMEM((hidden, features), BF),
            pltpu.VMEM((GROUP * pitch_in, LANES), F32),
            pltpu.VMEM((GROUP * pitch_out, LANES), F32),
            pltpu.SemaphoreType.DMA((3,)),
        ],
        compiler_params=pltpu.CompilerParams(vmem_limit_bytes=VMEM_LIMIT),
        cost_estimate=pl.CostEstimate(flops=flops, bytes_accessed=40_000_000, transcendentals=0),
    )(recv, gate_t, up_t, down)


def combine_kernel(tiles, pitch, routes_ref, gates_ref, in_ref, out_ref, score_ref, rows_ref, stage_ref):
    step = pl.program_id(0)
    features, tokens = out_ref.shape

    def store(j, r, c, value):
        rows_ref[r, c] = value

    unpack_rows(step, in_ref, stage_ref, store, 1, tiles, pitch)

    @pl.when(step == LANES // GROUP - 1)
    def _():
        named, _, rank = route_maps(routes_ref[...])
        gates = gates_ref[...]
        weight = functools.reduce(lambda a, b: a + b, [m * gates[k : k + 1, :] for k, m in enumerate(named)])
        mixed = jnp.concatenate([jnp.where(rank == float(s), weight, 0.0).T for s in range(SLOTS)], axis=1)
        high = mixed.astype(BF)
        low = (mixed - high.astype(F32)).astype(BF)
        both = jnp.concatenate([high, low], axis=0)
        for lo in range(0, features, 512):
            hi = min(lo + 512, features)
            part = jnp.dot(both, rows_ref[:, lo:hi], preferred_element_type=F32)
            part = part[:tokens] + part[tokens:]
            out_ref[lo:hi, :] = part.T.astype(BF)
        rest = features - (tiles - 1) * LANES
        last = rows_ref[:, (tiles - 1) * LANES :].astype(F32)
        score = last[:, rest : rest + 1] + last[:, rest + 1 : rest + 2]
        for k, m in enumerate(named):
            terms = [
                jnp.where(rank == float(s), m, 0.0) * score[s * LANES : (s + 1) * LANES]
                for s in range(SLOTS)
            ]
            score_ref[k : k + 1, :] = jnp.sum(
                functools.reduce(lambda a, b: a + b, terms), axis=0, keepdims=True
            )


def combine(routes_t, gates_t, recv, features):
    topk, tokens = routes_t.shape
    tiles = -(-features // LANES)
    rows = recv.shape[1]
    pitch = rows + 1
    return pl.pallas_call(
        functools.partial(combine_kernel, tiles, pitch),
        grid=(LANES // GROUP,),
        in_specs=[
            pl.BlockSpec(routes_t.shape, lambda i: (0, 0)),
            pl.BlockSpec(gates_t.shape, lambda i: (0, 0)),
            pl.BlockSpec((GROUP, rows, LANES), lambda i: (i, 0, 0)),
        ],
        out_specs=[
            pl.BlockSpec((features, tokens), lambda i: (0, 0)),
            pl.BlockSpec((topk, tokens), lambda i: (0, 0)),
        ],
        out_shape=[
            jax.ShapeDtypeStruct((features, tokens), BF),
            jax.ShapeDtypeStruct((topk, tokens), F32),
        ],
        scratch_shapes=[
            pltpu.VMEM((SLOTS * LANES, tiles * LANES), BF),
            pltpu.VMEM((GROUP * pitch, LANES), F32),
        ],
        compiler_params=pltpu.CompilerParams(vmem_limit_bytes=VMEM_LIMIT),
    )(routes_t, gates_t, recv)


def exchange(messages):
    return lax.all_to_all(messages, ("node", "local"), split_axis=0, concat_axis=0, tiled=True)


def shards(tokens, out_grad, routes, gates, w_gate, w_up, w_down):
    features = tokens.shape[1]
    routes_t, gates_t = routes.T, gates.T
    gate_t = jnp.swapaxes(w_gate, 1, 2)[0]
    up_t = jnp.swapaxes(w_up, 1, 2)[0]
    recv = exchange(dispatch(routes_t, tokens.T, out_grad.T))
    back = exchange(expert(recv, gate_t, up_t, w_down[0]))
    input_grad_t, gate_grad_t = combine(routes_t, gates_t, back, features)
    return (input_grad_t.T, gate_grad_t.T)


def solution(mesh):
    both = ("node", "local")
    return jax.shard_map(
        shards,
        mesh=mesh,
        in_specs=(P(both, None),) * 4 + (P(both, None, None),) * 3,
        out_specs=(P(both, None), P(both, None)),
        check_vma=False,
    )
```

```python
import functools

import jax
import jax.numpy as jnp
from jax import lax
from jax.experimental import pallas as pl
from jax.experimental.pallas import tpu as pltpu
from jax.sharding import PartitionSpec as P

LANES = 128
GROUP = 16
SLOTS = 5
PARTS = 4
BF = jnp.bfloat16
F32 = jnp.float32
NT = (((1,), (1,)), ((), ()))
VMEM_LIMIT = 60 * 1024 * 1024


def round_up(value, step):
    return -(-value // step) * step


def route_maps(routes_t):
    topk, tokens = routes_t.shape
    expert = lax.broadcasted_iota(jnp.int32, (LANES, tokens), 0)
    named = [jnp.where(routes_t[k : k + 1, :] == expert, 1.0, 0.0) for k in range(topk)]
    total = functools.reduce(lambda a, b: a + b, named)
    row = lax.broadcasted_iota(jnp.int32, (tokens, tokens), 0)
    column = lax.broadcasted_iota(jnp.int32, (tokens, tokens), 1)
    earlier = jnp.where(row < column, 1.0, 0.0).astype(BF)
    rank = jnp.dot(total.astype(BF), earlier, preferred_element_type=F32)
    return named, total, rank


def pack_messages(stage_ref, buffer_ref, rows, pitch, begin, end, finish):
    for first in range(begin, end, GROUP):
        for a in range(first, first + GROUP):
            buffer_ref[a, :rows] = stage_ref[a * pitch : a * pitch + rows, :].astype(BF)
        finish(first // GROUP)


def group_copies(source, target, sems):
    return [
        pltpu.make_async_copy(source(pl.ds(g * GROUP, GROUP)), target(pl.ds(g * GROUP, GROUP)), sems.at[g])
        for g in range(LANES // GROUP)
    ]


def dispatch_kernel(tiles, pitch, routes_ref, tok_ref, grad_ref, out_hbm, stage_ref, buffer_ref, sems):
    features = tok_ref.shape[0]
    peers, rows, _ = out_hbm.shape
    copies = group_copies(lambda g: buffer_ref.at[g], lambda g: out_hbm.at[g], sems)
    _, total, rank = route_maps(routes_ref[...])
    place = [jnp.where(rank == float(s), total, 0.0).astype(BF) for s in range(SLOTS)]

    def part_of(begin):
        count = peers // PARTS
        rows_of = jnp.concatenate([p[begin : begin + count] for p in place], axis=0)
        for j, ref in enumerate((tok_ref, grad_ref)):
            for lo in range(0, features, 256):
                hi = min(lo + 256, features)
                part = lax.dot_general(rows_of, ref[lo:hi, :], NT, preferred_element_type=F32)
                if (hi - lo) % LANES:
                    part = jnp.concatenate(
                        [part, jnp.zeros((part.shape[0], LANES - (hi - lo) % LANES), F32)], axis=1
                    )
                for s in range(SLOTS):
                    for t in range(part.shape[1] // LANES):
                        row = begin * pitch + (j * SLOTS + s) * tiles + lo // LANES + t
                        stage_ref[pl.ds(row, count, stride=pitch), :] = part[
                            s * count : (s + 1) * count, t * LANES : (t + 1) * LANES
                        ]

    for row in range(2 * SLOTS * tiles, rows):
        stage_ref[pl.ds(row, peers, stride=pitch), :] = jnp.zeros((peers, LANES), F32)
    for begin in range(0, peers, peers // PARTS):
        part_of(begin)
        pack_messages(
            stage_ref, buffer_ref, rows, pitch, begin, begin + peers // PARTS, lambda g: copies[g].start()
        )
    for copy in copies:
        copy.wait()


def dispatch(routes_t, tok_t, grad_t):
    features, tokens = tok_t.shape
    tiles = -(-features // LANES)
    rows = round_up(2 * SLOTS * tiles, 8)
    pitch = rows + 1
    return pl.pallas_call(
        functools.partial(dispatch_kernel, tiles, pitch),
        in_specs=[pl.BlockSpec(memory_space=pltpu.VMEM)] * 3,
        out_specs=pl.BlockSpec(memory_space=pl.ANY),
        out_shape=jax.ShapeDtypeStruct((LANES, rows, LANES), BF),
        scratch_shapes=[
            pltpu.VMEM((LANES * pitch, LANES), F32),
            pltpu.VMEM((LANES, rows, LANES), BF),
            pltpu.SemaphoreType.DMA((LANES // GROUP,)),
        ],
        compiler_params=pltpu.CompilerParams(vmem_limit_bytes=VMEM_LIMIT),
    )(routes_t, tok_t, grad_t)


def hidden_chunks(hidden):
    edges = [0, *range(256, hidden, 512), hidden]
    return list(zip(edges[:-1], edges[1:]))


def expert_kernel(
    tiles, pitch_in, pitch_out, in_hbm, gate_hbm, up_hbm, down_hbm, out_hbm,
    buffer_ref, rows_ref, pre_ref, upg_ref, gate_ref, up_ref, down_ref, stage_ref, in_sems, out_sems, w_sems,
):
    peers, rows_in, _ = in_hbm.shape
    rows_out = out_hbm.shape[1]
    hidden, features = gate_hbm.shape
    wide = SLOTS * peers
    arrivals = group_copies(lambda g: in_hbm.at[g], lambda g: buffer_ref.at[g], in_sems)
    departures = group_copies(
        lambda g: buffer_ref.at[g, pl.ds(0, rows_out)], lambda g: out_hbm.at[g], out_sems
    )
    chunks = hidden_chunks(hidden)
    weights = [
        [
            pltpu.make_async_copy(src.at[pl.ds(lo, hi - lo)], dst.at[pl.ds(lo, hi - lo)], w_sems.at[i, c])
            for i, (src, dst) in enumerate(((gate_hbm, gate_ref), (up_hbm, up_ref), (down_hbm, down_ref)))
        ]
        for c, (lo, hi) in enumerate(chunks)
    ]
    for copy in [*arrivals, *weights[0]]:
        copy.start()

    first_row = [0, (SLOTS * tiles) // 16 * 16]

    def unpack(j, g):
        start, count = first_row[j], rows_in - first_row[1]
        base = g * GROUP * pitch_out
        for a in range(GROUP):
            stage_ref[base + a * pitch_out : base + a * pitch_out + count, :] = buffer_ref[
                g * GROUP + a, start : start + count
            ].astype(F32)
        for s in range(SLOTS):
            for t in range(tiles):
                row = base + (j * SLOTS + s) * tiles + t - start
                value = stage_ref[pl.ds(row, GROUP, stride=pitch_out), :]
                first = s * peers + g * GROUP
                rows_ref[j, first : first + GROUP, t * LANES : (t + 1) * LANES] = value.astype(BF)

    for g, copy in enumerate(arrivals):
        copy.wait()
        unpack(0, g)

    score = jnp.zeros((wide, 1), F32)
    for c, (lo, hi) in enumerate(chunks):
        for copy in weights[c]:
            copy.wait()
        for copy in weights[c + 1] if c + 1 < len(chunks) else []:
            copy.start()
        x = rows_ref[0, :, :features]
        gate_pre = lax.dot_general(x, gate_ref[lo:hi, :], NT, preferred_element_type=F32)
        up_pre = lax.dot_general(x, up_ref[lo:hi, :], NT, preferred_element_type=F32)
        if c == 0:
            for g in range(len(arrivals)):
                unpack(1, g)
        hidden_grad = lax.dot_general(
            rows_ref[1, :, :features], down_ref[lo:hi, :], NT, preferred_element_type=F32
        )
        sig = jax.nn.sigmoid(gate_pre)
        act = gate_pre * sig
        act_up = (act * up_pre).astype(BF).astype(F32)
        score = score + jnp.sum(act_up * hidden_grad, axis=1, keepdims=True)
        upg_ref[:, lo:hi] = (hidden_grad * act).astype(BF)
        pre_ref[:, lo:hi] = (hidden_grad * up_pre * sig * (1.0 + gate_pre * (1.0 - sig))).astype(BF)
    high = score.astype(BF).astype(F32)
    low = score - high

    def place(value, row):
        for s in range(SLOTS):
            stage_ref[pl.ds(s * tiles + row, peers, stride=pitch_out), :] = value[
                s * peers : (s + 1) * peers
            ]

    def columns(lo, width):
        back = jnp.dot(pre_ref[...], gate_ref[:, pl.ds(lo, width)], preferred_element_type=F32)
        return back + jnp.dot(upg_ref[...], up_ref[:, pl.ds(lo, width)], preferred_element_type=F32)

    for row in range(SLOTS * tiles, rows_out):
        stage_ref[pl.ds(row, peers, stride=pitch_out), :] = jnp.zeros((peers, LANES), F32)
    whole = features // 256

    for n in range(whole):
        part = columns(n * 256, 256)
        place(part[:, :LANES], 2 * n)
        place(part[:, LANES:], 2 * n + 1)

    rest = features - whole * 256
    lane = lax.broadcasted_iota(jnp.int32, (wide, LANES - rest), 1)
    scores = jnp.where(lane == 0, high, jnp.where(lane == 1, low, 0.0))
    place(jnp.concatenate([columns(whole * 256, rest), scores], axis=1), 2 * whole)
    pack_messages(stage_ref, buffer_ref, rows_out, pitch_out, 0, peers, lambda g: departures[g].start())
    for copy in departures:
        copy.wait()


def expert(recv, gate_t, up_t, down):
    peers, rows_in, _ = recv.shape
    hidden, features = gate_t.shape
    tiles = -(-features // LANES)
    rows_out = round_up(SLOTS * tiles, 8)
    groups = LANES // GROUP
    pitch_in, pitch_out = rows_in + 1, rows_out + 1
    wide = SLOTS * LANES
    flops = 5 * 2 * wide * hidden * features
    return pl.pallas_call(
        functools.partial(expert_kernel, tiles, pitch_in, pitch_out),
        in_specs=[pl.BlockSpec(memory_space=pl.ANY)] * 4,
        out_specs=pl.BlockSpec(memory_space=pl.ANY),
        out_shape=jax.ShapeDtypeStruct((peers, rows_out, LANES), BF),
        scratch_shapes=[
            pltpu.VMEM((peers, rows_in, LANES), BF),
            pltpu.VMEM((2, wide, tiles * LANES), BF),
            pltpu.VMEM((wide, hidden), BF),
            pltpu.VMEM((wide, hidden), BF),
            pltpu.VMEM((hidden, features), BF),
            pltpu.VMEM((hidden, features), BF),
            pltpu.VMEM((hidden, features), BF),
            pltpu.VMEM((LANES * pitch_out, LANES), F32),
            pltpu.SemaphoreType.DMA((groups,)),
            pltpu.SemaphoreType.DMA((groups,)),
            pltpu.SemaphoreType.DMA((3, len(hidden_chunks(hidden)))),
        ],
        compiler_params=pltpu.CompilerParams(vmem_limit_bytes=VMEM_LIMIT),
        cost_estimate=pl.CostEstimate(flops=flops, bytes_accessed=40_000_000, transcendentals=0),
    )(recv, gate_t, up_t, down)


def combine_kernel(
    tiles, pitch, routes_ref, gates_ref, in_hbm, out_ref, score_ref, buffer_ref, stage_ref, sems
):
    features, tokens = out_ref.shape
    peers, rows, _ = in_hbm.shape
    arrivals = group_copies(lambda g: in_hbm.at[g], lambda g: buffer_ref.at[g], sems)
    for copy in arrivals:
        copy.start()
    named, _, rank = route_maps(routes_ref[...])
    gates = gates_ref[...]
    weight = functools.reduce(lambda a, b: a + b, [m * gates[k : k + 1, :] for k, m in enumerate(named)])
    mixed = jnp.concatenate([jnp.where(rank == float(s), weight, 0.0).T for s in range(SLOTS)], axis=1)
    high = mixed.astype(BF)
    low = (mixed - high.astype(F32)).astype(BF)
    both = jnp.concatenate([high, low], axis=0)
    for g, copy in enumerate(arrivals):
        copy.wait()
        for a in range(g * GROUP, (g + 1) * GROUP):
            stage_ref[a * pitch : a * pitch + rows, :] = buffer_ref[a].astype(F32)

    def tile(t):
        return [stage_ref[pl.ds(s * tiles + t, peers, stride=pitch), :] for s in range(SLOTS)]

    for first in range(0, tiles, 2):
        last = min(first + 2, tiles)
        columns = [jnp.concatenate(tile(t), axis=0).astype(BF) for t in range(first, last)]
        part = jnp.dot(both, jnp.concatenate(columns, axis=1), preferred_element_type=F32)
        part = (part[:tokens] + part[tokens:]).T.astype(BF)
        hi = min(last * LANES, features)
        out_ref[first * LANES : hi, :] = part[: hi - first * LANES]
    rest = features - (tiles - 1) * LANES
    scores = [end[:, rest : rest + 1] + end[:, rest + 1 : rest + 2] for end in tile(tiles - 1)]
    for k, m in enumerate(named):
        terms = [jnp.where(rank == float(s), m, 0.0) * scores[s] for s in range(SLOTS)]
        score_ref[k : k + 1, :] = jnp.sum(
            functools.reduce(lambda a, b: a + b, terms), axis=0, keepdims=True
        )


def combine(routes_t, gates_t, recv, features):
    topk, tokens = routes_t.shape
    tiles = -(-features // LANES)
    peers, rows, _ = recv.shape
    pitch = rows + 1
    vmem = pl.BlockSpec(memory_space=pltpu.VMEM)
    return pl.pallas_call(
        functools.partial(combine_kernel, tiles, pitch),
        in_specs=[vmem, vmem, pl.BlockSpec(memory_space=pl.ANY)],
        out_specs=[vmem, vmem],
        out_shape=[
            jax.ShapeDtypeStruct((features, tokens), BF),
            jax.ShapeDtypeStruct((topk, tokens), F32),
        ],
        scratch_shapes=[
            pltpu.VMEM((peers, rows, LANES), BF),
            pltpu.VMEM((peers * pitch, LANES), F32),
            pltpu.SemaphoreType.DMA((peers // GROUP,)),
        ],
        compiler_params=pltpu.CompilerParams(vmem_limit_bytes=VMEM_LIMIT),
    )(routes_t, gates_t, recv)


def exchange(messages):
    return lax.all_to_all(messages, ("node", "local"), split_axis=0, concat_axis=0, tiled=True)


def shards(tokens, out_grad, routes, gates, w_gate, w_up, w_down):
    features = tokens.shape[1]
    routes_t, gates_t = routes.T, gates.T
    gate_t = jnp.swapaxes(w_gate, 1, 2)[0]
    up_t = jnp.swapaxes(w_up, 1, 2)[0]
    recv = exchange(dispatch(routes_t, tokens.T, out_grad.T))
    back = exchange(expert(recv, gate_t, up_t, w_down[0]))
    input_grad_t, gate_grad_t = combine(routes_t, gates_t, back, features)
    return (input_grad_t.T, gate_grad_t.T)


def solution(mesh):
    both = ("node", "local")
    return jax.shard_map(
        shards,
        mesh=mesh,
        in_specs=(P(both, None),) * 4 + (P(both, None, None),) * 3,
        out_specs=(P(both, None), P(both, None)),
        check_vma=False,
    )
```

```python
import functools

import jax
import jax.numpy as jnp
from jax import lax
from jax.experimental import pallas as pl
from jax.experimental.pallas import tpu as pltpu
from jax.sharding import PartitionSpec as P

LANES = 128
GROUP = 16
SLOTS = 5
PARTS = 4
BF = jnp.bfloat16
F32 = jnp.float32
NT = (((1,), (1,)), ((), ()))
SMALL_LIMIT = 14 * 1024 * 1024
EXPERT_LIMIT = 33 * 1024 * 1024


def round_up(value, step):
    return -(-value // step) * step


def route_maps(routes_t):
    topk, tokens = routes_t.shape
    expert = lax.broadcasted_iota(jnp.int32, (LANES, tokens), 0)
    named = [jnp.where(routes_t[k : k + 1, :] == expert, 1.0, 0.0) for k in range(topk)]
    total = functools.reduce(lambda a, b: a + b, named)
    row = lax.broadcasted_iota(jnp.int32, (tokens, tokens), 0)
    column = lax.broadcasted_iota(jnp.int32, (tokens, tokens), 1)
    earlier = jnp.where(row < column, 1.0, 0.0).astype(BF)
    rank = jnp.dot(total.astype(BF), earlier, preferred_element_type=F32)
    return named, total, rank


def pack_messages(stage_ref, base, out_ref, rows, pitch, begin, end):
    for a in range(begin, end):
        first = base + (a - begin) * pitch
        out_ref[a] = stage_ref[first : first + rows, :].astype(BF)


def in_vmem(value):
    return pltpu.with_memory_space_constraint(value, pltpu.VMEM)


def dispatch_kernel(
    tiles, pitch, routes_hbm, tok_hbm, grad_hbm, out_ref, routes_ref, tok_ref, grad_ref, stage_ref, sems
):
    copies = [
        pltpu.make_async_copy(src, dst, sems.at[i])
        for i, (src, dst) in enumerate(
            ((routes_hbm, routes_ref), (tok_hbm, tok_ref), (grad_hbm, grad_ref))
        )
    ]
    for copy in copies:
        copy.start()
    copies[0].wait()
    features = tok_ref.shape[0]
    peers, rows, _ = out_ref.shape
    _, total, rank = route_maps(routes_ref[...])
    place = [jnp.where(rank == float(s), total, 0.0).astype(BF) for s in range(SLOTS)]

    def part_of(begin, base):
        rows_of = jnp.concatenate([p[begin : begin + count] for p in place], axis=0)
        for j, ref in enumerate((tok_ref, grad_ref)):
            for lo in range(0, features, 256):
                hi = min(lo + 256, features)
                part = lax.dot_general(rows_of, ref[lo:hi, :], NT, preferred_element_type=F32)
                if (hi - lo) % LANES:
                    part = jnp.concatenate(
                        [part, jnp.zeros((part.shape[0], LANES - (hi - lo) % LANES), F32)], axis=1
                    )
                for s in range(SLOTS):
                    for t in range(part.shape[1] // LANES):
                        row = base + (j * SLOTS + s) * tiles + lo // LANES + t
                        stage_ref[pl.ds(row, count, stride=pitch), :] = part[
                            s * count : (s + 1) * count, t * LANES : (t + 1) * LANES
                        ]

    count = peers // PARTS
    for row in range(2 * SLOTS * tiles, rows):
        stage_ref[pl.ds(row, 2 * count, stride=pitch), :] = jnp.zeros((2 * count, LANES), F32)
    copies[1].wait()
    copies[2].wait()
    for part in range(PARTS):
        base = part % 2 * count * pitch
        part_of(part * count, base)
        pack_messages(stage_ref, base, out_ref, rows, pitch, part * count, (part + 1) * count)


def dispatch(routes_t, tok_t, grad_t):
    features, tokens = tok_t.shape
    tiles = -(-features // LANES)
    rows = round_up(2 * SLOTS * tiles, 8)
    pitch = rows + 1
    return pl.pallas_call(
        functools.partial(dispatch_kernel, tiles, pitch),
        in_specs=[pl.BlockSpec(memory_space=pltpu.HBM)] * 3,
        out_specs=pl.BlockSpec(memory_space=pltpu.VMEM),
        out_shape=pltpu.VMEM((LANES, rows, LANES), BF),
        scratch_shapes=[
            pltpu.VMEM(routes_t.shape, routes_t.dtype),
            pltpu.VMEM(tok_t.shape, BF),
            pltpu.VMEM(grad_t.shape, BF),
            pltpu.VMEM((2 * LANES // PARTS * pitch, LANES), F32),
            pltpu.SemaphoreType.DMA((3,)),
        ],
        compiler_params=pltpu.CompilerParams(vmem_limit_bytes=SMALL_LIMIT),
    )(*[pltpu.with_memory_space_constraint(v, pltpu.HBM) for v in (routes_t, tok_t, grad_t)])


def expert_kernel(
    tiles, pitch_in, pitch_out, in_ref, gate_ref, up_ref, down_hbm, out_ref,
    rows_ref, pre_ref, upg_ref, down_ref, stage_ref, sem,
):
    peers, rows_in, _ = in_ref.shape
    rows_out = out_ref.shape[1]
    hidden, features = gate_ref.shape
    wide = SLOTS * peers
    chunks = [(lo, min(lo + 512, hidden)) for lo in range(0, hidden, 512)]
    arrival = pltpu.make_async_copy(down_hbm, down_ref, sem)
    arrival.start()
    first_row = [0, (SLOTS * tiles) // 16 * 16]

    def unpack(j, g):
        start, count = first_row[j], rows_in - first_row[1]
        base = g * GROUP * pitch_out
        for a in range(GROUP):
            stage_ref[base + a * pitch_out : base + a * pitch_out + count, :] = in_ref[
                g * GROUP + a, start : start + count
            ].astype(F32)
        for s in range(SLOTS):
            for t in range(tiles):
                row = base + (j * SLOTS + s) * tiles + t - start
                value = stage_ref[pl.ds(row, GROUP, stride=pitch_out), :]
                first = s * peers + g * GROUP
                rows_ref[j, first : first + GROUP, t * LANES : (t + 1) * LANES] = value.astype(BF)

    for g in range(peers // GROUP):
        unpack(0, g)

    score = jnp.zeros((wide, 1), F32)
    for c, (lo, hi) in enumerate(chunks):
        x = rows_ref[0, :, :features]
        gate_pre = lax.dot_general(x, gate_ref[lo:hi, :], NT, preferred_element_type=F32)
        up_pre = lax.dot_general(x, up_ref[lo:hi, :], NT, preferred_element_type=F32)
        if c == 0:
            for g in range(peers // GROUP):
                unpack(1, g)
            arrival.wait()
        hidden_grad = lax.dot_general(
            rows_ref[1, :, :features], down_ref[lo:hi, :], NT, preferred_element_type=F32
        )
        sig = jax.nn.sigmoid(gate_pre)
        act = gate_pre * sig
        act_up = (act * up_pre).astype(BF).astype(F32)
        score = score + jnp.sum(act_up * hidden_grad, axis=1, keepdims=True)
        upg_ref[:, lo:hi] = (hidden_grad * act).astype(BF)
        pre_ref[:, lo:hi] = (hidden_grad * up_pre * sig * (1.0 + gate_pre * (1.0 - sig))).astype(BF)
    high = score.astype(BF).astype(F32)
    low = score - high

    def place(value, row):
        for s in range(SLOTS):
            stage_ref[pl.ds(s * tiles + row, peers, stride=pitch_out), :] = value[
                s * peers : (s + 1) * peers
            ]

    def columns(lo, width):
        back = jnp.dot(pre_ref[...], gate_ref[:, pl.ds(lo, width)], preferred_element_type=F32)
        return back + jnp.dot(upg_ref[...], up_ref[:, pl.ds(lo, width)], preferred_element_type=F32)

    for row in range(SLOTS * tiles, rows_out):
        stage_ref[pl.ds(row, peers, stride=pitch_out), :] = jnp.zeros((peers, LANES), F32)
    whole = features // 256

    for n in range(whole):
        part = columns(n * 256, 256)
        place(part[:, :LANES], 2 * n)
        place(part[:, LANES:], 2 * n + 1)

    rest = features - whole * 256
    lane = lax.broadcasted_iota(jnp.int32, (wide, LANES - rest), 1)
    scores = jnp.where(lane == 0, high, jnp.where(lane == 1, low, 0.0))
    place(jnp.concatenate([columns(whole * 256, rest), scores], axis=1), 2 * whole)
    pack_messages(stage_ref, 0, out_ref, rows_out, pitch_out, 0, peers)


def expert(recv, gate_t, up_t, down):
    peers, rows_in, _ = recv.shape
    hidden, features = gate_t.shape
    tiles = -(-features // LANES)
    rows_out = round_up(SLOTS * tiles, 8)
    pitch_in, pitch_out = rows_in + 1, rows_out + 1
    wide = SLOTS * LANES
    flops = 5 * 2 * wide * hidden * features
    return pl.pallas_call(
        functools.partial(expert_kernel, tiles, pitch_in, pitch_out),
        in_specs=[pl.BlockSpec(memory_space=pltpu.VMEM)] * 3 + [pl.BlockSpec(memory_space=pl.ANY)],
        out_specs=pl.BlockSpec(memory_space=pltpu.VMEM),
        out_shape=pltpu.VMEM((peers, rows_out, LANES), BF),
        scratch_shapes=[
            pltpu.VMEM((2, wide, tiles * LANES), BF),
            pltpu.VMEM((wide, hidden), BF),
            pltpu.VMEM((wide, hidden), BF),
            pltpu.VMEM((hidden, features), BF),
            pltpu.VMEM((LANES * pitch_out, LANES), F32),
            pltpu.SemaphoreType.DMA,
        ],
        compiler_params=pltpu.CompilerParams(vmem_limit_bytes=EXPERT_LIMIT),
        cost_estimate=pl.CostEstimate(flops=flops, bytes_accessed=40_000_000, transcendentals=0),
    )(in_vmem(recv), in_vmem(gate_t), in_vmem(up_t), down)


def combine_kernel(
    tiles, pitch, routes_ref, gates_ref, in_ref, out_ref, score_ref, stage_ref
):
    features, tokens = out_ref.shape
    peers, rows, _ = in_ref.shape
    named, _, rank = route_maps(routes_ref[...])
    gates = gates_ref[...]
    weight = functools.reduce(lambda a, b: a + b, [m * gates[k : k + 1, :] for k, m in enumerate(named)])
    mixed = jnp.concatenate([jnp.where(rank == float(s), weight, 0.0).T for s in range(SLOTS)], axis=1)
    high = mixed.astype(BF)
    low = (mixed - high.astype(F32)).astype(BF)
    both = jnp.concatenate([high, low], axis=0)
    for a in range(peers):
        stage_ref[a * pitch : a * pitch + rows, :] = in_ref[a].astype(F32)

    def tile(t):
        return [stage_ref[pl.ds(s * tiles + t, peers, stride=pitch), :] for s in range(SLOTS)]

    for first in range(0, tiles, 2):
        last = min(first + 2, tiles)
        columns = [jnp.concatenate(tile(t), axis=0).astype(BF) for t in range(first, last)]
        part = jnp.dot(both, jnp.concatenate(columns, axis=1), preferred_element_type=F32)
        part = (part[:tokens] + part[tokens:]).T.astype(BF)
        hi = min(last * LANES, features)
        out_ref[first * LANES : hi, :] = part[: hi - first * LANES]
    rest = features - (tiles - 1) * LANES
    scores = [end[:, rest : rest + 1] + end[:, rest + 1 : rest + 2] for end in tile(tiles - 1)]
    for k, m in enumerate(named):
        terms = [jnp.where(rank == float(s), m, 0.0) * scores[s] for s in range(SLOTS)]
        score_ref[k : k + 1, :] = jnp.sum(
            functools.reduce(lambda a, b: a + b, terms), axis=0, keepdims=True
        )


def combine(routes_t, gates_t, recv, features):
    topk, tokens = routes_t.shape
    tiles = -(-features // LANES)
    peers, rows, _ = recv.shape
    pitch = rows + 1
    vmem = pl.BlockSpec(memory_space=pltpu.VMEM)
    return pl.pallas_call(
        functools.partial(combine_kernel, tiles, pitch),
        in_specs=[vmem, vmem, vmem],
        out_specs=[vmem, vmem],
        out_shape=[
            jax.ShapeDtypeStruct((features, tokens), BF),
            jax.ShapeDtypeStruct((topk, tokens), F32),
        ],
        scratch_shapes=[
            pltpu.VMEM((peers * pitch, LANES), F32),
        ],
        compiler_params=pltpu.CompilerParams(vmem_limit_bytes=SMALL_LIMIT),
    )(routes_t, gates_t, in_vmem(recv))


def exchange(messages):
    return lax.all_to_all(messages, ("node", "local"), split_axis=0, concat_axis=0, tiled=True)


def shards(tokens, out_grad, routes, gates, w_gate, w_up, w_down):
    features = tokens.shape[1]
    routes_t, gates_t = routes.T, gates.T
    gate_t = jnp.swapaxes(w_gate, 1, 2)[0]
    up_t = jnp.swapaxes(w_up, 1, 2)[0]
    send = dispatch(routes_t, tokens.T, out_grad.T)
    send, gate_t, up_t = lax.optimization_barrier((send, gate_t, up_t))
    recv = exchange(send)
    back = exchange(expert(recv, gate_t, up_t, w_down[0]))
    input_grad_t, gate_grad_t = combine(routes_t, gates_t, back, features)
    return (input_grad_t.T, gate_grad_t.T)


def solution(mesh):
    both = ("node", "local")
    return jax.shard_map(
        shards,
        mesh=mesh,
        in_specs=(P(both, None),) * 4 + (P(both, None, None),) * 3,
        out_specs=(P(both, None), P(both, None)),
        check_vma=False,
    )
```

```python
import functools

import jax
import jax.numpy as jnp
from jax import lax
from jax.experimental import pallas as pl
from jax.experimental.pallas import tpu as pltpu
from jax.sharding import PartitionSpec as P

LANES = 128
GROUP = 16
SLOTS = 5
FOLD = 2
BLOCK = 128
HALF = LANES // 2
PARTS = 4
BF = jnp.bfloat16
F32 = jnp.float32
NT = (((1,), (1,)), ((), ()))
SMALL_LIMIT = 14 * 1024 * 1024
EXPERT_LIMIT = 33 * 1024 * 1024


def round_up(value, step):
    return -(-value // step) * step


def route_maps(routes_t):
    topk, tokens = routes_t.shape
    expert = lax.broadcasted_iota(jnp.int32, (LANES, tokens), 0)
    named = [jnp.where(routes_t[k : k + 1, :] == expert, 1.0, 0.0) for k in range(topk)]
    total = functools.reduce(lambda a, b: a + b, named)
    row = lax.broadcasted_iota(jnp.int32, (tokens, tokens), 0)
    column = lax.broadcasted_iota(jnp.int32, (tokens, tokens), 1)
    earlier = jnp.where(row < column, 1.0, 0.0).astype(BF)
    rank = jnp.dot(total.astype(BF), earlier, preferred_element_type=F32)
    return named, total, rank


def pack_messages(stage_ref, base, out_ref, rows, pitch, begin, end):
    for a in range(begin, end):
        first = base + (a - begin) * pitch
        out_ref[a] = stage_ref[first : first + rows, :].astype(BF)


def copy_rows(source_ref, target_ref, kind):
    for row in range(0, source_ref.shape[0], BLOCK):
        target_ref[row : row + BLOCK, :] = source_ref[row : row + BLOCK, :].astype(kind)


def in_vmem(value):
    return pltpu.with_memory_space_constraint(value, pltpu.VMEM)


def dispatch_kernel(
    tiles, pitch, routes_hbm, tok_hbm, grad_hbm, out_ref, routes_ref, tok_ref, grad_ref, stage_ref, sems
):
    copies = [
        pltpu.make_async_copy(src, dst, sems.at[i])
        for i, (src, dst) in enumerate(
            ((routes_hbm, routes_ref), (tok_hbm, tok_ref), (grad_hbm, grad_ref))
        )
    ]
    for copy in copies:
        copy.start()
    copies[0].wait()
    features = tok_ref.shape[0]
    peers, rows, _ = out_ref.shape
    _, total, rank = route_maps(routes_ref[...])
    place = [jnp.where(rank == float(s), total, 0.0).astype(BF) for s in range(SLOTS)]

    def part_of(begin, base):
        rows_of = jnp.concatenate([p[begin : begin + count] for p in place], axis=0)
        for j, ref in enumerate((tok_ref, grad_ref)):
            for lo in range(0, features, 256):
                hi = min(lo + 256, features)
                part = lax.dot_general(rows_of, ref[lo:hi, :], NT, preferred_element_type=F32)
                if (hi - lo) % LANES:
                    part = jnp.concatenate(
                        [part, jnp.zeros((part.shape[0], LANES - (hi - lo) % LANES), F32)], axis=1
                    )
                for s in range(SLOTS):
                    for t in range(part.shape[1] // LANES):
                        row = base + (j * SLOTS + s) * tiles + lo // LANES + t
                        stage_ref[pl.ds(row, count, stride=pitch), :] = part[
                            s * count : (s + 1) * count, t * LANES : (t + 1) * LANES
                        ]

    count = peers // PARTS
    for row in range(2 * SLOTS * tiles, rows):
        stage_ref[pl.ds(row, 2 * count, stride=pitch), :] = jnp.zeros((2 * count, LANES), F32)
    copies[1].wait()
    copies[2].wait()
    for part in range(PARTS):
        base = part % 2 * count * pitch
        part_of(part * count, base)
        pack_messages(stage_ref, base, out_ref, rows, pitch, part * count, (part + 1) * count)


def dispatch(routes_t, tok_t, grad_t):
    features, tokens = tok_t.shape
    tiles = -(-features // LANES)
    rows = round_up(2 * SLOTS * tiles, 8)
    pitch = rows + 1
    return pl.pallas_call(
        functools.partial(dispatch_kernel, tiles, pitch),
        in_specs=[pl.BlockSpec(memory_space=pltpu.HBM)] * 3,
        out_specs=pl.BlockSpec(memory_space=pltpu.VMEM),
        out_shape=pltpu.VMEM((LANES, rows, LANES), BF),
        scratch_shapes=[
            pltpu.VMEM(routes_t.shape, routes_t.dtype),
            pltpu.VMEM(tok_t.shape, BF),
            pltpu.VMEM(grad_t.shape, BF),
            pltpu.VMEM((2 * LANES // PARTS * pitch, LANES), F32),
            pltpu.SemaphoreType.DMA((3,)),
        ],
        compiler_params=pltpu.CompilerParams(vmem_limit_bytes=SMALL_LIMIT),
    )(*[pltpu.with_memory_space_constraint(v, pltpu.HBM) for v in (routes_t, tok_t, grad_t)])


def expert_kernel(
    tiles, pitch_in, pitch_out, in_ref, gate_ref, up_ref, down_hbm, out_ref,
    rows_ref, pre_ref, upg_ref, down_ref, stage_ref, sem,
):
    peers, rows_in, _ = in_ref.shape
    rows_out = out_ref.shape[0] // peers
    hidden, features = gate_ref.shape
    wide = SLOTS * peers
    chunks = [(lo, min(lo + 512, hidden)) for lo in range(0, hidden, 512)]
    arrival = pltpu.make_async_copy(down_hbm, down_ref, sem)
    arrival.start()
    whole = features // LANES
    first_row = [0, (SLOTS * tiles) // 16 * 16]

    def unpack(j, g):
        start, count = first_row[j], rows_in - first_row[1]
        pitch = count + 1
        base = g * GROUP * pitch
        for a in range(GROUP):
            stage_ref[base + a * pitch : base + a * pitch + count, :] = in_ref[
                g * GROUP + a, start : start + count
            ].astype(F32)
        for s in range(SLOTS):
            for t in range(tiles):
                row = base + (j * SLOTS + s) * tiles + t - start
                value = stage_ref[pl.ds(row, GROUP, stride=pitch), :]
                first = s * peers + g * GROUP
                rows_ref[j, first : first + GROUP, t * LANES : (t + 1) * LANES] = value.astype(BF)

    for g in range(peers // GROUP):
        unpack(0, g)

    score = jnp.zeros((wide, 1), F32)
    for c, (lo, hi) in enumerate(chunks):
        x = rows_ref[0, :, :features]
        gate_pre = lax.dot_general(x, gate_ref[lo:hi, :], NT, preferred_element_type=F32)
        up_pre = lax.dot_general(x, up_ref[lo:hi, :], NT, preferred_element_type=F32)
        if c == 0:
            for g in range(peers // GROUP):
                unpack(1, g)
            arrival.wait()
        hidden_grad = lax.dot_general(
            rows_ref[1, :, :features], down_ref[lo:hi, :], NT, preferred_element_type=F32
        )
        sig = jax.nn.sigmoid(gate_pre)
        act = gate_pre * sig
        act_up = (act * up_pre).astype(BF).astype(F32)
        score = score + jnp.sum(act_up * hidden_grad, axis=1, keepdims=True)
        upg_ref[:, lo:hi] = (hidden_grad * act).astype(BF)
        pre_ref[:, lo:hi] = (hidden_grad * up_pre * sig * (1.0 + gate_pre * (1.0 - sig))).astype(BF)
    high = score.astype(BF).astype(F32)
    low = score - high

    def place(value, s, t):
        stage_ref[pl.ds(s * whole + t, peers, stride=pitch_out), :] = value

    def columns(lo, width):
        back = jnp.dot(pre_ref[...], gate_ref[:, pl.ds(lo, width)], preferred_element_type=F32)
        return back + jnp.dot(upg_ref[...], up_ref[:, pl.ds(lo, width)], preferred_element_type=F32)

    for lo in range(0, whole * LANES, 256):
        part = columns(lo, 256)
        for s in range(SLOTS):
            for t in range(2):
                place(part[s * peers : (s + 1) * peers, t * LANES : (t + 1) * LANES], s, lo // LANES + t)
    part = columns(whole * LANES, HALF)
    lane = lax.broadcasted_iota(jnp.int32, (peers, HALF), 1)
    halves = [part[s * peers : (s + 1) * peers] for s in range(SLOTS)]
    scores = jnp.zeros((peers, HALF), F32)
    for s in range(SLOTS):
        rows = slice(s * peers, (s + 1) * peers)
        scores = jnp.where(lane == 2 * s, high[rows], jnp.where(lane == 2 * s + 1, low[rows], scores))
    halves.append(scores)
    for pair in range(len(halves) // 2):
        place(jnp.concatenate(halves[2 * pair : 2 * pair + 2], axis=1), SLOTS, pair)
    for row in range(SLOTS * whole + len(halves) // 2, rows_out):
        place(jnp.zeros((peers, LANES), F32), 0, row)
    for row in range(0, out_ref.shape[0], BLOCK):
        out_ref[row : row + BLOCK, :] = stage_ref[row : row + BLOCK, :].astype(BF)


def expert(recv, gate_t, up_t, down):
    peers, rows_in, _ = recv.shape
    hidden, features = gate_t.shape
    tiles = -(-features // LANES)
    rows_out = round_up(SLOTS * (tiles - 1) + (SLOTS + 1) // 2, FOLD)
    pitch_in, pitch_out = rows_in + 1, rows_out
    wide = SLOTS * LANES
    flops = 5 * 2 * wide * hidden * features
    return pl.pallas_call(
        functools.partial(expert_kernel, tiles, pitch_in, pitch_out),
        in_specs=[pl.BlockSpec(memory_space=pltpu.VMEM)] * 3 + [pl.BlockSpec(memory_space=pl.ANY)],
        out_specs=pl.BlockSpec(memory_space=pltpu.VMEM),
        out_shape=pltpu.VMEM((peers * rows_out, LANES), BF),
        scratch_shapes=[
            pltpu.VMEM((2, wide, tiles * LANES), BF),
            pltpu.VMEM((wide, hidden), BF),
            pltpu.VMEM((wide, hidden), BF),
            pltpu.VMEM((hidden, features), BF),
            pltpu.VMEM((LANES * (rows_out + 7), LANES), F32),
            pltpu.SemaphoreType.DMA,
        ],
        compiler_params=pltpu.CompilerParams(vmem_limit_bytes=EXPERT_LIMIT),
        cost_estimate=pl.CostEstimate(flops=flops, bytes_accessed=40_000_000, transcendentals=0),
    )(in_vmem(recv), in_vmem(gate_t), in_vmem(up_t), down)


def combine_kernel(
    tiles, pitch, routes_ref, gates_ref, in_ref, out_ref, score_ref, stage_ref
):
    features, tokens = out_ref.shape
    peers = LANES
    named, _, rank = route_maps(routes_ref[...])
    gates = gates_ref[...]
    weight = functools.reduce(lambda a, b: a + b, [m * gates[k : k + 1, :] for k, m in enumerate(named)])
    mixed = jnp.concatenate([jnp.where(rank == float(s), weight, 0.0).T for s in range(SLOTS)], axis=1)
    high = mixed.astype(BF)
    low = (mixed - high.astype(F32)).astype(BF)
    both = jnp.concatenate([high, low], axis=0)
    copy_rows(in_ref, stage_ref, F32)
    whole = tiles - 1
    pairs = [
        stage_ref[pl.ds(SLOTS * whole + pair, peers, stride=pitch), :] for pair in range((SLOTS + 1) // 2)
    ]
    ends = [pairs[s // 2] if s % 2 == 0 else pltpu.roll(pairs[s // 2], HALF, 1) for s in range(SLOTS + 1)]

    def tile(t):
        if t == whole:
            return ends[:SLOTS]
        return [stage_ref[pl.ds(s * whole + t, peers, stride=pitch), :] for s in range(SLOTS)]

    for first in range(0, tiles, 2):
        last = min(first + 2, tiles)
        columns = [jnp.concatenate(tile(t), axis=0).astype(BF) for t in range(first, last)]
        part = jnp.dot(both, jnp.concatenate(columns, axis=1), preferred_element_type=F32)
        part = (part[:tokens] + part[tokens:]).T.astype(BF)
        hi = min(last * LANES, features)
        out_ref[first * LANES : hi, :] = part[: hi - first * LANES]
    scores = [ends[-1][:, 2 * s : 2 * s + 1] + ends[-1][:, 2 * s + 1 : 2 * s + 2] for s in range(SLOTS)]
    for k, m in enumerate(named):
        terms = [jnp.where(rank == float(s), m, 0.0) * scores[s] for s in range(SLOTS)]
        score_ref[k : k + 1, :] = jnp.sum(
            functools.reduce(lambda a, b: a + b, terms), axis=0, keepdims=True
        )


def combine(routes_t, gates_t, recv, features):
    topk, tokens = routes_t.shape
    tiles = -(-features // LANES)
    pitch = recv.shape[0] // LANES
    vmem = pl.BlockSpec(memory_space=pltpu.VMEM)
    return pl.pallas_call(
        functools.partial(combine_kernel, tiles, pitch),
        in_specs=[vmem, vmem, vmem],
        out_specs=[vmem, vmem],
        out_shape=[
            jax.ShapeDtypeStruct((features, tokens), BF),
            jax.ShapeDtypeStruct((topk, tokens), F32),
        ],
        scratch_shapes=[
            pltpu.VMEM(recv.shape, F32),
        ],
        compiler_params=pltpu.CompilerParams(vmem_limit_bytes=SMALL_LIMIT),
    )(routes_t, gates_t, in_vmem(recv))


def exchange(messages):
    return lax.all_to_all(messages, ("node", "local"), split_axis=0, concat_axis=0, tiled=True)


def shards(tokens, out_grad, routes, gates, w_gate, w_up, w_down):
    features = tokens.shape[1]
    routes_t, gates_t = routes.T, gates.T
    gate_t = jnp.swapaxes(w_gate, 1, 2)[0]
    up_t = jnp.swapaxes(w_up, 1, 2)[0]
    send = dispatch(routes_t, tokens.T, out_grad.T)
    send, gate_t, up_t = lax.optimization_barrier((send, gate_t, up_t))
    recv = exchange(send)
    back = expert(recv, gate_t, up_t, w_down[0])
    peers = recv.shape[0]
    rows = back.shape[0] // peers
    back = exchange(back.reshape(peers, rows // FOLD, FOLD, LANES)).reshape(back.shape)
    input_grad_t, gate_grad_t = combine(routes_t, gates_t, back, features)
    return (input_grad_t.T, gate_grad_t.T)


def solution(mesh):
    both = ("node", "local")
    return jax.shard_map(
        shards,
        mesh=mesh,
        in_specs=(P(both, None),) * 4 + (P(both, None, None),) * 3,
        out_specs=(P(both, None), P(both, None)),
        check_vma=False,
    )
```

```python
import functools

import jax
import jax.numpy as jnp
from jax import lax
from jax.experimental import pallas as pl
from jax.experimental.pallas import tpu as pltpu
from jax.sharding import PartitionSpec as P

LANES = 128
GROUP = 16
SLOTS = 5
FOLD = 2
BLOCK = 128
HALF = LANES // 2
PARTS = 4
BF = jnp.bfloat16
F32 = jnp.float32
NT = (((1,), (1,)), ((), ()))
SMALL_LIMIT = 14 * 1024 * 1024
EXPERT_LIMIT = 33 * 1024 * 1024


def round_up(value, step):
    return -(-value // step) * step


def route_maps(routes_t):
    topk, tokens = routes_t.shape
    expert = lax.broadcasted_iota(jnp.int32, (LANES, tokens), 0)
    named = [jnp.where(routes_t[k : k + 1, :] == expert, 1.0, 0.0) for k in range(topk)]
    total = functools.reduce(lambda a, b: a + b, named)
    row = lax.broadcasted_iota(jnp.int32, (tokens, tokens), 0)
    column = lax.broadcasted_iota(jnp.int32, (tokens, tokens), 1)
    earlier = jnp.where(row < column, 1.0, 0.0).astype(BF)
    rank = jnp.dot(total.astype(BF), earlier, preferred_element_type=F32)
    return named, total, rank


def pack_messages(stage_ref, base, out_ref, rows, pitch, begin, end):
    for a in range(begin, end):
        first = base + (a - begin) * pitch
        out_ref[a] = stage_ref[first : first + rows, :].astype(BF)


def copy_rows(source_ref, target_ref, kind):
    for row in range(0, source_ref.shape[0], BLOCK):
        target_ref[row : row + BLOCK, :] = source_ref[row : row + BLOCK, :].astype(kind)


def in_vmem(value):
    return pltpu.with_memory_space_constraint(value, pltpu.VMEM)


def dispatch_kernel(
    tiles, pitch, routes_hbm, tok_hbm, grad_hbm, out_ref, routes_ref, tok_ref, grad_ref, stage_ref, sems
):
    copies = [
        pltpu.make_async_copy(src, dst, sems.at[i])
        for i, (src, dst) in enumerate(
            ((routes_hbm, routes_ref), (tok_hbm, tok_ref), (grad_hbm, grad_ref))
        )
    ]
    for copy in copies:
        copy.start()
    copies[0].wait()
    features = tok_ref.shape[0]
    peers, rows, _ = out_ref.shape
    _, total, rank = route_maps(routes_ref[...])
    place = [jnp.where(rank == float(s), total, 0.0).astype(BF) for s in range(SLOTS)]

    def part_of(begin, base):
        rows_of = jnp.concatenate([p[begin : begin + count] for p in place], axis=0)
        for j, ref in enumerate((tok_ref, grad_ref)):
            for lo in range(0, features, 256):
                hi = min(lo + 256, features)
                part = lax.dot_general(rows_of, ref[lo:hi, :], NT, preferred_element_type=F32)
                if (hi - lo) % LANES:
                    part = jnp.concatenate(
                        [part, jnp.zeros((part.shape[0], LANES - (hi - lo) % LANES), F32)], axis=1
                    )
                for s in range(SLOTS):
                    for t in range(part.shape[1] // LANES):
                        row = base + (j * SLOTS + s) * tiles + lo // LANES + t
                        stage_ref[pl.ds(row, count, stride=pitch), :] = part[
                            s * count : (s + 1) * count, t * LANES : (t + 1) * LANES
                        ]

    count = peers // PARTS
    for row in range(2 * SLOTS * tiles, rows):
        stage_ref[pl.ds(row, 2 * count, stride=pitch), :] = jnp.zeros((2 * count, LANES), F32)
    copies[1].wait()
    copies[2].wait()
    for part in range(PARTS):
        base = part % 2 * count * pitch
        part_of(part * count, base)
        pack_messages(stage_ref, base, out_ref, rows, pitch, part * count, (part + 1) * count)


def dispatch(routes_t, tok_t, grad_t):
    features, tokens = tok_t.shape
    tiles = -(-features // LANES)
    rows = round_up(2 * SLOTS * tiles, 8)
    pitch = rows + 1
    return pl.pallas_call(
        functools.partial(dispatch_kernel, tiles, pitch),
        in_specs=[pl.BlockSpec(memory_space=pltpu.HBM)] * 3,
        out_specs=pl.BlockSpec(memory_space=pltpu.VMEM),
        out_shape=pltpu.VMEM((LANES, rows, LANES), BF),
        scratch_shapes=[
            pltpu.VMEM(routes_t.shape, routes_t.dtype),
            pltpu.VMEM(tok_t.shape, BF),
            pltpu.VMEM(grad_t.shape, BF),
            pltpu.VMEM((2 * LANES // PARTS * pitch, LANES), F32),
            pltpu.SemaphoreType.DMA((3,)),
        ],
        compiler_params=pltpu.CompilerParams(vmem_limit_bytes=SMALL_LIMIT),
    )(*[pltpu.with_memory_space_constraint(v, pltpu.HBM) for v in (routes_t, tok_t, grad_t)])


def expert_kernel(
    tiles, pitch_in, pitch_out, in_ref, gate_ref, up_ref, down_hbm, out_ref,
    rows_ref, pre_ref, upg_ref, down_ref, stage_ref, sems,
):
    peers, rows_in, _ = in_ref.shape
    rows_out = out_ref.shape[0] // peers
    hidden, features = gate_ref.shape
    wide = SLOTS * peers
    chunks = [(lo, min(lo + 512, hidden)) for lo in range(0, hidden, 512)]
    arrivals = [
        pltpu.make_async_copy(down_hbm.at[pl.ds(lo, hi - lo)], down_ref.at[pl.ds(lo, hi - lo)], sems.at[c])
        for c, (lo, hi) in enumerate(chunks)
    ]
    for arrival in arrivals:
        arrival.start()
    whole = features // LANES
    first_row = [0, (SLOTS * tiles) // 16 * 16]

    def unpack(j, g):
        start, count = first_row[j], rows_in - first_row[1]
        pitch = count + 1
        base = g * GROUP * pitch
        for a in range(GROUP):
            stage_ref[base + a * pitch : base + a * pitch + count, :] = in_ref[
                g * GROUP + a, start : start + count
            ].astype(F32)
        for s in range(SLOTS):
            for t in range(tiles):
                row = base + (j * SLOTS + s) * tiles + t - start
                value = stage_ref[pl.ds(row, GROUP, stride=pitch), :]
                first = s * peers + g * GROUP
                rows_ref[j, first : first + GROUP, t * LANES : (t + 1) * LANES] = value.astype(BF)

    for g in range(peers // GROUP):
        unpack(0, g)

    score = jnp.zeros((wide, 1), F32)
    for c, (lo, hi) in enumerate(chunks):
        x = rows_ref[0, :, :features]
        gate_pre = lax.dot_general(x, gate_ref[lo:hi, :], NT, preferred_element_type=F32)
        up_pre = lax.dot_general(x, up_ref[lo:hi, :], NT, preferred_element_type=F32)
        if c == 0:
            for g in range(peers // GROUP):
                unpack(1, g)
        arrivals[c].wait()
        hidden_grad = lax.dot_general(
            rows_ref[1, :, :features], down_ref[lo:hi, :], NT, preferred_element_type=F32
        )
        sig = jax.nn.sigmoid(gate_pre)
        act = gate_pre * sig
        act_up = (act * up_pre).astype(BF).astype(F32)
        score = score + jnp.sum(act_up * hidden_grad, axis=1, keepdims=True)
        upg_ref[:, lo:hi] = (hidden_grad * act).astype(BF)
        pre_ref[:, lo:hi] = (hidden_grad * up_pre * sig * (1.0 + gate_pre * (1.0 - sig))).astype(BF)
    high = score.astype(BF).astype(F32)
    low = score - high

    def place(value, s, t):
        stage_ref[pl.ds(s * whole + t, peers, stride=pitch_out), :] = value

    def columns(lo, width):
        back = jnp.dot(pre_ref[...], gate_ref[:, pl.ds(lo, width)], preferred_element_type=F32)
        return back + jnp.dot(upg_ref[...], up_ref[:, pl.ds(lo, width)], preferred_element_type=F32)

    for lo in range(0, whole * LANES, 256):
        part = columns(lo, 256)
        for s in range(SLOTS):
            for t in range(2):
                place(part[s * peers : (s + 1) * peers, t * LANES : (t + 1) * LANES], s, lo // LANES + t)
    part = columns(whole * LANES, HALF)
    lane = lax.broadcasted_iota(jnp.int32, (peers, HALF), 1)
    halves = [part[s * peers : (s + 1) * peers] for s in range(SLOTS)]
    scores = jnp.zeros((peers, HALF), F32)
    for s in range(SLOTS):
        rows = slice(s * peers, (s + 1) * peers)
        scores = jnp.where(lane == 2 * s, high[rows], jnp.where(lane == 2 * s + 1, low[rows], scores))
    halves.append(scores)
    for pair in range(len(halves) // 2):
        place(jnp.concatenate(halves[2 * pair : 2 * pair + 2], axis=1), SLOTS, pair)
    for row in range(SLOTS * whole + len(halves) // 2, rows_out):
        place(jnp.zeros((peers, LANES), F32), 0, row)
    for row in range(0, out_ref.shape[0], BLOCK):
        out_ref[row : row + BLOCK, :] = stage_ref[row : row + BLOCK, :].astype(BF)


def expert(recv, gate_t, up_t, down):
    peers, rows_in, _ = recv.shape
    hidden, features = gate_t.shape
    tiles = -(-features // LANES)
    rows_out = round_up(SLOTS * (tiles - 1) + (SLOTS + 1) // 2, FOLD)
    pitch_in, pitch_out = rows_in + 1, rows_out
    wide = SLOTS * LANES
    flops = 5 * 2 * wide * hidden * features
    return pl.pallas_call(
        functools.partial(expert_kernel, tiles, pitch_in, pitch_out),
        in_specs=[pl.BlockSpec(memory_space=pltpu.VMEM)] * 3 + [pl.BlockSpec(memory_space=pl.ANY)],
        out_specs=pl.BlockSpec(memory_space=pltpu.VMEM),
        out_shape=pltpu.VMEM((peers * rows_out, LANES), BF),
        scratch_shapes=[
            pltpu.VMEM((2, wide, tiles * LANES), BF),
            pltpu.VMEM((wide, hidden), BF),
            pltpu.VMEM((wide, hidden), BF),
            pltpu.VMEM((hidden, features), BF),
            pltpu.VMEM((LANES * (rows_out + 7), LANES), F32),
            pltpu.SemaphoreType.DMA((-(-hidden // 512),)),
        ],
        compiler_params=pltpu.CompilerParams(vmem_limit_bytes=EXPERT_LIMIT),
        cost_estimate=pl.CostEstimate(flops=flops, bytes_accessed=40_000_000, transcendentals=0),
    )(in_vmem(recv), in_vmem(gate_t), in_vmem(up_t), down)


def combine_kernel(
    tiles, pitch, routes_ref, gates_ref, in_ref, out_ref, score_ref, stage_ref
):
    features, tokens = out_ref.shape
    peers = LANES
    named, _, rank = route_maps(routes_ref[...])
    gates = gates_ref[...]
    weight = functools.reduce(lambda a, b: a + b, [m * gates[k : k + 1, :] for k, m in enumerate(named)])
    mixed = jnp.concatenate([jnp.where(rank == float(s), weight, 0.0).T for s in range(SLOTS)], axis=1)
    high = mixed.astype(BF)
    low = (mixed - high.astype(F32)).astype(BF)
    both = jnp.concatenate([high, low], axis=0)
    copy_rows(in_ref, stage_ref, F32)
    whole = tiles - 1
    pairs = [
        stage_ref[pl.ds(SLOTS * whole + pair, peers, stride=pitch), :] for pair in range((SLOTS + 1) // 2)
    ]
    ends = [pairs[s // 2] if s % 2 == 0 else pltpu.roll(pairs[s // 2], HALF, 1) for s in range(SLOTS + 1)]

    def tile(t):
        if t == whole:
            return ends[:SLOTS]
        return [stage_ref[pl.ds(s * whole + t, peers, stride=pitch), :] for s in range(SLOTS)]

    for first in range(0, tiles, 2):
        last = min(first + 2, tiles)
        columns = [jnp.concatenate(tile(t), axis=0).astype(BF) for t in range(first, last)]
        part = jnp.dot(both, jnp.concatenate(columns, axis=1), preferred_element_type=F32)
        part = (part[:tokens] + part[tokens:]).T.astype(BF)
        hi = min(last * LANES, features)
        out_ref[first * LANES : hi, :] = part[: hi - first * LANES]
    scores = [ends[-1][:, 2 * s : 2 * s + 1] + ends[-1][:, 2 * s + 1 : 2 * s + 2] for s in range(SLOTS)]
    for k, m in enumerate(named):
        terms = [jnp.where(rank == float(s), m, 0.0) * scores[s] for s in range(SLOTS)]
        score_ref[k : k + 1, :] = jnp.sum(
            functools.reduce(lambda a, b: a + b, terms), axis=0, keepdims=True
        )


def combine(routes_t, gates_t, recv, features):
    topk, tokens = routes_t.shape
    tiles = -(-features // LANES)
    pitch = recv.shape[0] // LANES
    vmem = pl.BlockSpec(memory_space=pltpu.VMEM)
    return pl.pallas_call(
        functools.partial(combine_kernel, tiles, pitch),
        in_specs=[vmem, vmem, vmem],
        out_specs=[vmem, vmem],
        out_shape=[
            jax.ShapeDtypeStruct((features, tokens), BF),
            jax.ShapeDtypeStruct((topk, tokens), F32),
        ],
        scratch_shapes=[
            pltpu.VMEM(recv.shape, F32),
        ],
        compiler_params=pltpu.CompilerParams(vmem_limit_bytes=SMALL_LIMIT),
    )(routes_t, gates_t, in_vmem(recv))


def exchange(messages):
    return lax.all_to_all(messages, ("node", "local"), split_axis=0, concat_axis=0, tiled=True)


def shards(tokens, out_grad, routes, gates, w_gate, w_up, w_down):
    features = tokens.shape[1]
    routes_t, gates_t = routes.T, gates.T
    gate_t = jnp.swapaxes(w_gate, 1, 2)[0]
    up_t = jnp.swapaxes(w_up, 1, 2)[0]
    send = dispatch(routes_t, tokens.T, out_grad.T)
    send, gate_t, up_t = lax.optimization_barrier((send, gate_t, up_t))
    recv = exchange(send)
    back = expert(recv, gate_t, up_t, w_down[0])
    peers = recv.shape[0]
    rows = back.shape[0] // peers
    back = exchange(back.reshape(peers, rows // FOLD, FOLD, LANES)).reshape(back.shape)
    input_grad_t, gate_grad_t = combine(routes_t, gates_t, back, features)
    return (input_grad_t.T, gate_grad_t.T)


def solution(mesh):
    both = ("node", "local")
    return jax.shard_map(
        shards,
        mesh=mesh,
        in_specs=(P(both, None),) * 4 + (P(both, None, None),) * 3,
        out_specs=(P(both, None), P(both, None)),
        check_vma=False,
    )
```
